256 devices in a mesh: row: 16 (over y_hi, z), col: 4 (over y_lo, core), ka: 4 (over x).
Axes of the slice: x: 4, y: 4 (y_hi: 2, y_lo: 2; y = y_hi * 2 + y_lo), z: 8, core: 2. Of those that a mesh axis runs over, the one named last changes fastest.
Arguments:
- density: bfloat16 [4096, 4096], P('row', ('col', 'ka')), may hold values from -0.375 to 0.375
- pattern_start: int32 [16, 16], replicated, may hold values from 0 to 1, as said below
- pattern_square: int32 [16, 16], replicated, may hold values from 0 to 1, as said below
Outputs:
- purified: bfloat16 [4096, 4096], P('row', ('col', 'ka'))
The draws below stay inside these ranges and needn't reach their ends.
Inputs may be any that keep to these rules, and one draw needn't show every extreme that they name: `pattern_start`: symmetric 0/1 pattern with ones on the diagonal; the share of ones varies strongly between block rows. `pattern_square`: symmetric 0/1 pattern with ones on the diagonal; the share of ones varies strongly between block rows.
All inputs are finite; a program needn't handle non-finite values.
Results may differ from the reference program's by a relative error of at most 0.0048.
Values may be sent and summed in bfloat16 or wider, within the bound.
A program may use at most 64 MiB of HBM per device.

```python
import jax
import jax.numpy as jnp
from jax import lax

BLOCK = 256
STEPS = 2
NB = 16
ORDER = 4096


def make_pattern(key, lowest, highest):
    key_rows, key_cells = jax.random.split(key)
    levels = jax.random.randint(key_rows, (NB, 1), lowest, highest)
    scores = jax.random.randint(key_cells, (NB, NB), 0, 100)
    kept_cells = (scores < levels).astype(jnp.int32)
    symmetric = jnp.maximum(kept_cells, kept_cells.T)
    diagonal = (lax.broadcasted_iota(jnp.int32, (NB, NB), 0) == lax.broadcasted_iota(jnp.int32, (NB, NB), 1)).astype(jnp.int32)
    return jnp.maximum(symmetric, diagonal)


def draw_pattern_start(key, part):
    key = jax.random.fold_in(key, 1)
    return make_pattern(key, 5, 30)


def draw_pattern_square(key, part):
    key = jax.random.fold_in(key, 2)
    return make_pattern(key, 15, 50)


def block_scale(key, dims, cuts, smallest, largest):
    def one(position, blocks):
        draws = jax.random.uniform(jax.random.fold_in(jax.random.fold_in(key, 6), position), (blocks,), jnp.float32, smallest / len(cuts), largest / len(cuts))
        return jnp.repeat(jnp.exp(draws), dims[position] // blocks).reshape((-1,) + (1,) * (len(dims) - position - 1))

    level = one(*cuts[0])
    for cut in cuts[1:]:
        level = level * one(*cut)
    return level


def centred(key, dims, spread, reach, shards=(), kind=jnp.bfloat16):
    result = jax.random.normal(key, dims, jnp.float32) * spread
    if len(shards) > 0:
        result = block_scale(key, dims, shards, -0.22, 0.18) * result
    return jnp.clip(result, min=-reach, max=reach).astype(kind)


def setup_inputs(seed: int = 0) -> dict:
    key_of = jax.random.split(jax.random.key(seed), 4)
    density = centred(key_of[0], (ORDER, ORDER), (ORDER // 16) ** -0.5, 0.375, ((0, 16), (1, 16)))
    pattern_start = draw_pattern_start(jax.random.fold_in(key_of[3], 71), 0)
    pattern_square = draw_pattern_square(jax.random.fold_in(key_of[3], 71), 0)
    return {"density": density, "pattern_start": pattern_start, "pattern_square": pattern_square}


def expand_mask(pattern):
    full = jnp.broadcast_to(pattern[:, None, :, None], (NB, BLOCK, NB, BLOCK))
    return full.reshape(ORDER, ORDER) == 1


def reference(density, pattern_start, pattern_square):
    current = jnp.where(expand_mask(pattern_start), density, jnp.zeros_like(density))
    keep_square = expand_mask(pattern_square)
    for section in range(STEPS):
        square = jnp.dot(current, current.T, preferred_element_type=jnp.float32)
        square = jnp.where(keep_square, square, jnp.float32(0.0))
        if section % 2 == 0:
            following = 2.0 * current.astype(jnp.float32) - square
        else:
            following = square
        current = following.astype(jnp.bfloat16)
    return current
```

```python
import functools

import jax
import jax.numpy as jnp
from jax import lax
from jax.experimental import pallas as pl
from jax.experimental.pallas import tpu as pltpu
from jax.sharding import PartitionSpec as P

BLOCK = 256
HALF = 128
STEPS = 2
MESH = pl.DeviceIdType.MESH
HALVES = ((0, HALF), (HALF, HALF))


def select_block(flag, values):
    kept = jnp.full(values.shape, flag, jnp.int32) == 1
    return jnp.where(kept, values, jnp.zeros_like(values))


def kernel(
    start_ref, square_ref, density_ref, out_ref,
    left_own, left_sib, right_own, right_sib, outgoing, incoming, swapped,
    z_send, z_recv, sib_send, sib_recv, far_send, far_recv, sum_send, sum_recv, swap_send, swap_recv,
):
    row, col, x = lax.axis_index("row"), lax.axis_index("col"), lax.axis_index("ka")
    yh, z = row // 8, lax.rem(row, 8)
    yl, core = col // 2, lax.rem(col, 2)

    def device(yh_, yl_, z_, core_, x_):
        return (yh_ * 8 + z_, yl_ * 2 + core_, x_)

    sibling = device(yh, yl, z, 1 - core, x)
    up = device(yh, yl, lax.rem(z + 1, 8), core, x)
    down = device(yh, yl, lax.rem(z + 7, 8), core, x)
    across = device(yl, yh, z, core, x)
    far = (device(1 - yh, yl, z, core, x), device(yh, 1 - yl, z, core, x))

    barrier = pltpu.get_barrier_semaphore()
    partners = [sibling, up, down, device(1 - yh, 1 - yl, z, core, x)]
    for dx in range(4):
        there = lax.rem(x + dx, 4)
        partners.append(device(1 - yh, yl, z, core, there))
        partners.append(device(yh, 1 - yl, z, core, there))
        if dx:
            partners.append(device(yh, yl, z, core, there))
    for partner in partners:
        pl.semaphore_signal(barrier, inc=1, device_id=partner, device_id_type=MESH)

    left_own[0, :BLOCK] = select_block(
        start_ref[row, col * 4 + x], density_ref[...]
    )
    pl.semaphore_wait(barrier, len(partners))

    def remote(src, dst, send, recv, target):
        return pltpu.make_async_remote_copy(
            src_ref=src, dst_ref=dst, send_sem=send, recv_sem=recv,
            device_id=target, device_id_type=MESH,
        )

    def ring_copy(step, slot, half):
        first, count = HALVES[half]
        downward = slot < 4 or (slot == 4 and half == 0)
        origin = slot - 1 if downward else (slot + 1) % 8
        here = pl.ds(first, count)
        src = left_own.at[step, here] if origin == 0 else right_own.at[step, origin, here]
        return remote(
            src, right_own.at[step, slot, here],
            z_send.at[step, slot, half], z_recv.at[step, slot, half],
            down if downward else up,
        )

    def sib_copy(step, slot, half):
        here = pl.ds(*HALVES[half])
        return remote(
            right_own.at[step, slot, here], right_sib.at[step, slot, here],
            sib_send.at[step, slot, half], sib_recv.at[step, slot, half], sibling,
        )

    def sib_left(step, part):
        here = pl.ds(part * BLOCK, BLOCK)
        return remote(
            left_own.at[step, here], left_sib.at[step, here],
            sib_send.at[step, 0, part], sib_recv.at[step, 0, part], sibling,
        )

    def far_copy(step):
        return remote(
            left_own.at[step, pl.ds(0, BLOCK)], left_own.at[step, pl.ds(BLOCK, BLOCK)],
            far_send.at[step], far_recv.at[step], far[step],
        )

    swap = remote(left_own.at[0, pl.ds(0, BLOCK)], swapped, swap_send, swap_recv, across)

    def owner(step, pair, part):
        x_ = lax.rem(z + pair, 4)
        if step == 0:
            y_ = yh if part == 0 else 1 - yh
            slot = jnp.where(y_ == yl, 0, 4) + lax.rem(x - x_ + 4, 4)
            return device(yh, y_, z, core, x_), slot
        y_ = yl if part == 0 else 1 - yl
        slot = jnp.where(y_ == yh, 0, 4) + lax.rem(x - x_ + 4, 4)
        return device(y_, yl, z, core, x_), slot

    def sum_copy(step, pair, part):
        target, slot = owner(step, pair, part)
        return remote(
            outgoing.at[step, pair, part], incoming.at[step, slot],
            sum_send.at[step, pair, part], sum_recv.at[step, slot], target,
        ), slot

    def multiply(step, slot):
        pair = slot % 4
        if slot:
            own, sib = right_own[step, slot], right_sib[step, slot]
        else:
            own, sib = left_own[step, :BLOCK], left_sib[step, :BLOCK]
        dims = (((1,), (1,)), ((), ()))
        product = lax.dot_general(left_own[step], own, dims, preferred_element_type=jnp.float32)
        product += lax.dot_general(left_sib[step], sib, dims, preferred_element_type=jnp.float32)
        product = product.astype(jnp.bfloat16)
        for part in range(2):
            outgoing[step, pair, part] = product[part * BLOCK:(part + 1) * BLOCK]
            copy, where = sum_copy(step, pair, part)

            @pl.when(where != 0)
            def _():
                copy.start()

    def consume(step, slot):
        @pl.when(lax.rem(z + slot, 8) // 4 == core)
        def _():
            multiply(step, slot)

    for step in range(STEPS):
        if step == 0:
            row_, block_ = yl * 8 + z, yh * 8 + core * 4 + x
        else:
            row_, block_ = row, col * 4 + x
        for slot, half in ((1, 0), (7, 1), (1, 1), (7, 0)):
            ring_copy(step, slot, half).start()
        far_copy(step).start()
        sib_left(step, 0).start()
        if step == 0:
            @pl.when(yh != yl)
            def _():
                swap.start()

            @pl.when(yh == yl)
            def _():
                swapped[...] = left_own[0, :BLOCK]

        for stage in range(1, 5):
            if stage < 4:
                arrivals = ((stage, 0), (8 - stage, 1), (stage, 1), (8 - stage, 0))
            else:
                arrivals = ((4, 0), (4, 1))
            for slot, half in arrivals:
                ring_copy(step, slot, half).wait_recv()
                if slot < 3 or (slot == 3 and half == 0):
                    ring_copy(step, slot + 1, half).start()
                if slot > 5 or (slot == 5 and half == 1):
                    ring_copy(step, slot - 1, half).start()
                sib_copy(step, slot, half).start()
            if stage == 1:
                far_copy(step).wait_recv()
                sib_left(step, 1).start()
                sib_left(step, 0).wait_recv()
                sib_left(step, 1).wait_recv()
                consume(step, 0)
            else:
                for slot in (stage - 1, 9 - stage):
                    for half in range(2):
                        sib_copy(step, slot, half).wait_recv()
                    consume(step, slot)
        for half in range(2):
            sib_copy(step, 4, half).wait_recv()
        consume(step, 4)

        mine = lax.rem(x - z + 8, 4)
        part_ = jnp.where(yh == yl, 0, 1)
        total = outgoing[step, mine, part_].astype(jnp.float32)
        for slot in range(1, 8):
            remote(
                outgoing.at[step, 0, 0], incoming.at[step, slot],
                sum_send.at[step, 0, 0], sum_recv.at[step, slot], sibling,
            ).wait_recv()
            total += incoming[step, slot].astype(jnp.float32)
        square = select_block(square_ref[row_, block_], total)
        if step == 0:
            @pl.when(yh != yl)
            def _():
                swap.wait_recv()

            following = 2.0 * swapped[...].astype(jnp.float32) - square
            left_own[1, :BLOCK] = following.astype(jnp.bfloat16)
        else:
            out_ref[...] = square.astype(jnp.bfloat16)

    for step in range(STEPS):
        for slot in range(1, 8):
            for half in range(2):
                ring_copy(step, slot, half).wait_send()
                sib_copy(step, slot, half).wait_send()
        far_copy(step).wait_send()
        for part in range(2):
            sib_left(step, part).wait_send()
        for pair in range(4):
            for part in range(2):
                copy, where = sum_copy(step, pair, part)

                @pl.when(where != 0)
                def _():
                    copy.wait_send()

    @pl.when(yh != yl)
    def _():
        swap.wait_send()


def local(density, pattern_start, pattern_square):
    block = (BLOCK, BLOCK)
    kind = jnp.bfloat16
    dma = pltpu.SemaphoreType.DMA
    return pl.pallas_call(
        kernel,
        name="purify",
        out_shape=jax.ShapeDtypeStruct(block, kind),
        in_specs=[
            pl.BlockSpec(memory_space=pltpu.SMEM),
            pl.BlockSpec(memory_space=pltpu.SMEM),
            pl.BlockSpec(memory_space=pltpu.VMEM),
        ],
        out_specs=pl.BlockSpec(memory_space=pltpu.VMEM),
        scratch_shapes=[
            pltpu.VMEM((STEPS, 2 * BLOCK, BLOCK), kind),
            pltpu.VMEM((STEPS, 2 * BLOCK, BLOCK), kind),
            pltpu.VMEM((STEPS, 8) + block, kind),
            pltpu.VMEM((STEPS, 8) + block, kind),
            pltpu.VMEM((STEPS, 4, 2) + block, kind),
            pltpu.VMEM((STEPS, 8) + block, kind),
            pltpu.VMEM(block, kind),
            dma((STEPS, 8, 2)), dma((STEPS, 8, 2)),
            dma((STEPS, 8, 2)), dma((STEPS, 8, 2)),
            dma((STEPS,)), dma((STEPS,)),
            dma((STEPS, 4, 2)), dma((STEPS, 8)),
            dma(()), dma(()),
        ],
        compiler_params=pltpu.CompilerParams(
            collective_id=0, has_side_effects=True, vmem_limit_bytes=40 * 2**20
        ),
    )(pattern_start, pattern_square, density)


def solution(mesh):
    return jax.shard_map(
        local,
        mesh=mesh,
        in_specs=(P("row", ("col", "ka")), P(), P()),
        out_specs=P("row", ("col", "ka")),
        check_vma=False,
    )
```

```python
import functools

import jax
import jax.numpy as jnp
from jax import lax
from jax.experimental import pallas as pl
from jax.experimental.pallas import tpu as pltpu
from jax.sharding import PartitionSpec as P

BLOCK = 256
CHUNKS = 4
CHUNK = BLOCK // CHUNKS
HALF = BLOCK // 2
STEPS = 2
MESH = pl.DeviceIdType.MESH


def select_block(flag, values):
    kept = jnp.full(values.shape, flag, jnp.int32) == 1
    return jnp.where(kept, values, jnp.zeros_like(values))


def order(stage):
    near = range(CHUNKS // 2)
    rest = range(CHUNKS // 2, CHUNKS)
    if stage == 4:
        pairs = [((4, c), (4, c + CHUNKS // 2)) for c in near]
    else:
        pairs = [((stage, c), (8 - stage, d)) for c, d in zip([*near, *rest], [*rest, *near])]
    return [item for pair in pairs for item in pair]


def kernel(
    start_hbm, square_hbm, density_hbm, out_ref,
    density_ref, start_ref, square_ref, load_sem, left_own, left_sib, right_own, right_sib, outgoing, incoming, swapped,
    z_send, z_recv, sib_send, sib_recv, far_send, far_recv, sum_send, sum_recv, swap_send, swap_recv,
):
    row, col, x = lax.axis_index("row"), lax.axis_index("col"), lax.axis_index("ka")
    yh, z = row // 8, lax.rem(row, 8)
    yl, core = col // 2, lax.rem(col, 2)

    def device(yh_, yl_, z_, core_, x_):
        return (yh_ * 8 + z_, yl_ * 2 + core_, x_)

    sibling = device(yh, yl, z, 1 - core, x)
    up = device(yh, yl, lax.rem(z + 1, 8), core, x)
    down = device(yh, yl, lax.rem(z + 7, 8), core, x)
    across = device(yl, yh, z, core, x)
    far = (device(1 - yh, yl, z, core, x), device(yh, 1 - yl, z, core, x))

    loads = [
        pltpu.make_async_copy(src, dst, load_sem.at[i])
        for i, (src, dst) in enumerate(
            ((density_hbm, density_ref), (start_hbm, start_ref), (square_hbm, square_ref))
        )
    ]
    for load in loads:
        load.start()

    barrier = pltpu.get_barrier_semaphore()
    partners = [sibling, up, down, device(1 - yh, 1 - yl, z, core, x)]
    for dx in range(4):
        there = lax.rem(x + dx, 4)
        partners.append(device(1 - yh, yl, z, core, there))
        partners.append(device(yh, 1 - yl, z, core, there))
        if dx:
            partners.append(device(yh, yl, z, core, there))
    for partner in partners:
        pl.semaphore_signal(barrier, inc=1, device_id=partner, device_id_type=MESH)

    for load in loads:
        load.wait()
    left_own[0, :BLOCK] = select_block(
        start_ref[row, col * 4 + x], density_ref[...]
    )
    pl.semaphore_wait(barrier, len(partners))

    def remote(src, dst, send, recv, target):
        return pltpu.make_async_remote_copy(
            src_ref=src, dst_ref=dst, send_sem=send, recv_sem=recv,
            device_id=target, device_id_type=MESH,
        )

    def ring_copy(step, slot, chunk):
        downward = slot < 4 or (slot == 4 and chunk < CHUNKS // 2)
        origin = slot - 1 if downward else (slot + 1) % 8
        here = pl.ds(chunk * CHUNK, CHUNK)
        src = left_own.at[step, here] if origin == 0 else right_own.at[step, origin, here]
        return remote(
            src, right_own.at[step, slot, here],
            z_send.at[step, slot, chunk], z_recv.at[step, slot, chunk],
            down if downward else up,
        )

    def sib_copy(step, slot, half):
        here = pl.ds(half * HALF, HALF)
        return remote(
            right_own.at[step, slot, here], right_sib.at[step, slot, here],
            sib_send.at[step, slot, half], sib_recv.at[step, slot, half], sibling,
        )

    def sib_left(step, part):
        here = pl.ds(part * BLOCK, BLOCK)
        return remote(
            left_own.at[step, here], left_sib.at[step, here],
            sib_send.at[step, 0, part], sib_recv.at[step, 0, part], sibling,
        )

    def far_copy(step):
        return remote(
            left_own.at[step, pl.ds(0, BLOCK)], left_own.at[step, pl.ds(BLOCK, BLOCK)],
            far_send.at[step], far_recv.at[step], far[step],
        )

    swap = remote(left_own.at[0, pl.ds(0, BLOCK)], swapped, swap_send, swap_recv, across)

    def owner(step, pair, part):
        x_ = lax.rem(z + pair, 4)
        if step == 0:
            y_ = yh if part == 0 else 1 - yh
            slot = jnp.where(y_ == yl, 0, 4) + lax.rem(x - x_ + 4, 4)
            return device(yh, y_, z, core, x_), slot
        y_ = yl if part == 0 else 1 - yl
        slot = jnp.where(y_ == yh, 0, 4) + lax.rem(x - x_ + 4, 4)
        return device(y_, yl, z, core, x_), slot

    def sum_copy(step, pair, part):
        target, slot = owner(step, pair, part)
        return remote(
            outgoing.at[step, pair, part], incoming.at[step, slot],
            sum_send.at[step, pair, part], sum_recv.at[step, slot], target,
        ), slot

    def multiply(step, slot):
        pair = slot % 4
        if slot:
            own, sib = right_own[step, slot], right_sib[step, slot]
        else:
            own, sib = left_own[step, :BLOCK], left_sib[step, :BLOCK]
        dims = (((1,), (1,)), ((), ()))
        product = lax.dot_general(left_own[step], own, dims, preferred_element_type=jnp.float32)
        product += lax.dot_general(left_sib[step], sib, dims, preferred_element_type=jnp.float32)
        product = product.astype(jnp.bfloat16)
        for part in range(2):
            outgoing[step, pair, part] = product[part * BLOCK:(part + 1) * BLOCK]
            copy, where = sum_copy(step, pair, part)

            @pl.when(where != 0)
            def _():
                copy.start()

    def consume(step, slot):
        @pl.when(lax.rem(z + slot, 8) // 4 == core)
        def _():
            multiply(step, slot)

    for step in range(STEPS):
        if step == 0:
            row_, block_ = yl * 8 + z, yh * 8 + core * 4 + x
        else:
            row_, block_ = row, col * 4 + x
        for slot, chunk in order(1):
            ring_copy(step, slot, chunk).start()
        far_copy(step).start()
        sib_left(step, 0).start()
        if step == 0:
            @pl.when(yh != yl)
            def _():
                swap.start()

            @pl.when(yh == yl)
            def _():
                swapped[...] = left_own[0, :BLOCK]

        for stage in range(1, 5):
            for slot, chunk in order(stage):
                ring_copy(step, slot, chunk).wait_recv()
                if stage < 3 or (stage == 3 and (slot == 3) == (chunk < CHUNKS // 2)):
                    ring_copy(step, slot + 1 if slot < 4 else slot - 1, chunk).start()
                if chunk % (CHUNKS // 2) == CHUNKS // 2 - 1:
                    sib_copy(step, slot, chunk // (CHUNKS // 2)).start()
            if stage == 1:
                far_copy(step).wait_recv()
                sib_left(step, 1).start()
                sib_left(step, 0).wait_recv()
                sib_left(step, 1).wait_recv()
                consume(step, 0)
            for slot in (stage, 8 - stage) if stage < 4 else (4,):
                for half in range(2):
                    sib_copy(step, slot, half).wait_recv()
                consume(step, slot)

        mine = lax.rem(x - z + 8, 4)
        part_ = jnp.where(yh == yl, 0, 1)
        total = outgoing[step, mine, part_].astype(jnp.float32)
        for slot in range(1, 8):
            remote(
                outgoing.at[step, 0, 0], incoming.at[step, slot],
                sum_send.at[step, 0, 0], sum_recv.at[step, slot], sibling,
            ).wait_recv()
            total += incoming[step, slot].astype(jnp.float32)
        square = select_block(square_ref[row_, block_], total)
        if step == 0:
            @pl.when(yh != yl)
            def _():
                swap.wait_recv()

            following = 2.0 * swapped[...].astype(jnp.float32) - square
            left_own[1, :BLOCK] = following.astype(jnp.bfloat16)
        else:
            out_ref[...] = square.astype(jnp.bfloat16)

    for step in range(STEPS):
        for slot in range(1, 8):
            for chunk in range(CHUNKS):
                ring_copy(step, slot, chunk).wait_send()
            for half in range(2):
                sib_copy(step, slot, half).wait_send()
        far_copy(step).wait_send()
        for part in range(2):
            sib_left(step, part).wait_send()
        for pair in range(4):
            for part in range(2):
                copy, where = sum_copy(step, pair, part)

                @pl.when(where != 0)
                def _():
                    copy.wait_send()

    @pl.when(yh != yl)
    def _():
        swap.wait_send()


def local(density, pattern_start, pattern_square):
    block = (BLOCK, BLOCK)
    kind = jnp.bfloat16
    dma = pltpu.SemaphoreType.DMA
    return pl.pallas_call(
        kernel,
        name="purify",
        out_shape=jax.ShapeDtypeStruct(block, kind),
        in_specs=[
            pl.BlockSpec(memory_space=pl.ANY),
            pl.BlockSpec(memory_space=pl.ANY),
            pl.BlockSpec(memory_space=pl.ANY),
        ],
        out_specs=pl.BlockSpec(memory_space=pltpu.VMEM),
        scratch_shapes=[
            pltpu.VMEM(block, kind),
            pltpu.SMEM(pattern_start.shape, jnp.int32),
            pltpu.SMEM(pattern_square.shape, jnp.int32),
            dma((3,)),
            pltpu.VMEM((STEPS, 2 * BLOCK, BLOCK), kind),
            pltpu.VMEM((STEPS, 2 * BLOCK, BLOCK), kind),
            pltpu.VMEM((STEPS, 8) + block, kind),
            pltpu.VMEM((STEPS, 8) + block, kind),
            pltpu.VMEM((STEPS, 4, 2) + block, kind),
            pltpu.VMEM((STEPS, 8) + block, kind),
            pltpu.VMEM(block, kind),
            dma((STEPS, 8, CHUNKS)), dma((STEPS, 8, CHUNKS)),
            dma((STEPS, 8, 2)), dma((STEPS, 8, 2)),
            dma((STEPS,)), dma((STEPS,)),
            dma((STEPS, 4, 2)), dma((STEPS, 8)),
            dma(()), dma(()),
        ],
        compiler_params=pltpu.CompilerParams(
            collective_id=0, has_side_effects=True, vmem_limit_bytes=62 * 2**20
        ),
    )(pattern_start, pattern_square, density)


def solution(mesh):
    return jax.shard_map(
        local,
        mesh=mesh,
        in_specs=(P("row", ("col", "ka")), P(), P()),
        out_specs=P("row", ("col", "ka")),
        check_vma=False,
    )
```

```python
import jax
import jax.numpy as jnp
from jax import lax
from jax.experimental import pallas as pl
from jax.experimental.pallas import tpu as pltpu
from jax.sharding import PartitionSpec as P

BLOCK = 256
HALF = BLOCK // 2
STEPS = 2
MESH = pl.DeviceIdType.MESH


def select_block(flag, values):
    kept = jnp.full(values.shape, flag, jnp.int32) == 1
    return jnp.where(kept, values, jnp.zeros_like(values))


def order(stage):
    if stage == 4:
        return ((4, 0), (4, 1))
    return ((stage, 0), (8 - stage, 1), (stage, 1), (8 - stage, 0))


def kernel(
    start_hbm, square_hbm, density_hbm, out_ref,
    density_ref, start_ref, square_ref, load_sem, left, right, outgoing, incoming, swapped,
    z_send, z_recv, sib_send, sib_recv, far_send, far_recv, sum_send, sum_recv, swap_send, swap_recv,
):
    row, col, x = lax.axis_index("row"), lax.axis_index("col"), lax.axis_index("ka")
    yh, z = row // 8, lax.rem(row, 8)
    yl, core = col // 2, lax.rem(col, 2)

    def device(yh_, yl_, z_, core_, x_):
        return (yh_ * 8 + z_, yl_ * 2 + core_, x_)

    above, below = lax.rem(z + 1, 8), lax.rem(z + 7, 8)
    sibling = device(yh, yl, z, 1 - core, x)
    across = device(yl, yh, z, core, x)

    def over_yh(step):
        return yh + (1 - step) * (1 - 2 * yh)

    def over_yl(step):
        return yl + step * (1 - 2 * yl)

    loads = [
        pltpu.make_async_copy(src, dst, load_sem.at[i])
        for i, (src, dst) in enumerate(
            ((density_hbm, density_ref), (start_hbm, start_ref), (square_hbm, square_ref))
        )
    ]
    for load in loads:
        load.start()

    barrier = pltpu.get_barrier_semaphore()
    partners = [sibling, device(1 - yh, 1 - yl, z, core, x)]
    for z_ in (above, below):
        partners += [device(yh, yl, z_, core, x), device(yh, yl, z_, 1 - core, x)]
    for dx in range(4):
        there = lax.rem(x + dx, 4)
        partners.append(device(1 - yh, yl, z, core, there))
        partners.append(device(yh, 1 - yl, z, core, there))
        if dx:
            partners.append(device(yh, yl, z, core, there))
    for partner in partners:
        pl.semaphore_signal(barrier, inc=1, device_id=partner, device_id_type=MESH)

    for load in loads:
        load.wait()
    left[0, 0, :BLOCK] = select_block(start_ref[row, col * 4 + x], density_ref[...])
    pl.semaphore_wait(barrier, len(partners))

    def remote(src, dst, send, recv, target):
        return pltpu.make_async_remote_copy(
            src_ref=src, dst_ref=dst, send_sem=send, recv_sem=recv,
            device_id=target, device_id_type=MESH,
        )

    def user(z_, slot):
        return lax.rem(z_ + slot, 8) // 4

    def rows(half):
        return pl.ds(half * HALF, HALF)

    def ring_copy(step, slot, half):
        downward = slot < 4 or (slot == 4 and half == 0)
        origin = slot - 1 if downward else (slot + 1) % 8
        z_ = below if downward else above
        core_ = user(z_, 4) if slot == 4 else core
        lane = jnp.where(core_ == core, 0, 1) if slot == 4 else 0
        src = left.at[step, 0, rows(half)] if origin == 0 else right.at[step, 0, origin, rows(half)]
        return remote(
            src, right.at[step, lane, slot, rows(half)],
            z_send.at[step, slot, half], z_recv.at[step, lane, slot, half],
            device(yh, yl, z_, core_, x),
        )

    def ring_arrival(step, lane, slot, half):
        here = right.at[step, lane, slot, rows(half)]
        return remote(here, here, z_send.at[step, slot, half], z_recv.at[step, lane, slot, half], sibling)

    def sib_copy(step, slot, half):
        return remote(
            right.at[step, 0, slot, rows(half)], right.at[step, 1, slot, rows(half)],
            sib_send.at[step, slot, half], sib_recv.at[step, slot, half], sibling,
        )

    def sib_left(step, part):
        here = pl.ds(part * BLOCK, BLOCK)
        return remote(
            left.at[step, 0, here], left.at[step, 1, here],
            sib_send.at[step, 0, part], sib_recv.at[step, 0, part], sibling,
        )

    def far_copy(step):
        return remote(
            left.at[step, 0, pl.ds(0, BLOCK)], left.at[step, 0, pl.ds(BLOCK, BLOCK)],
            far_send.at[step], far_recv.at[step],
            device(over_yh(step), over_yl(step), z, core, x),
        )

    swap = remote(left.at[0, 0, pl.ds(0, BLOCK)], swapped, swap_send, swap_recv, across)

    def sum_copy(step, pair, crossing, half):
        x_ = lax.rem(z + pair, 4)
        slot = 4 * crossing + lax.rem(x - x_ + 4, 4)
        target = device(
            jnp.where(crossing != 0, over_yh(1 - step), yh),
            jnp.where(crossing != 0, over_yl(1 - step), yl), z, core, x_,
        )
        return remote(
            outgoing.at[step, pair, crossing, rows(half)], incoming.at[step, slot, rows(half)],
            sum_send.at[step, pair, crossing, half], sum_recv.at[step, slot, half], target,
        )

    def elsewhere(pair):
        return lax.rem(z + pair, 4) != x

    def multiply_part(step, slot, part):
        pair = slot % 4
        crossing = jnp.where(yh == yl, part, 1 - part)
        dims = (((1,), (1,)), ((), ()))
        here = pl.ds(part * BLOCK, BLOCK)
        product = jnp.zeros((BLOCK, BLOCK), jnp.float32)
        for lane in range(2):
            other = right[step, lane, slot] if slot else left[step, lane, :BLOCK]
            product += lax.dot_general(
                left[step, lane, here], other, dims, preferred_element_type=jnp.float32
            )
        outgoing[step, pair, crossing] = product.astype(jnp.bfloat16)

        @pl.when(jnp.logical_or(crossing != 0, elsewhere(pair)))
        def _():
            for half in range(2):
                sum_copy(step, pair, crossing, half).start()

    def multiply(step, slot):
        @pl.when(yh == yl)
        def _():
            for part in (1, 0):
                multiply_part(step, slot, part)

        @pl.when(yh != yl)
        def _():
            for part in (0, 1):
                multiply_part(step, slot, part)

    for slot, half in order(1):
        ring_copy(0, slot, half).start()

    @pl.when(yh != yl)
    def _():
        swap.start()

    @pl.when(yh == yl)
    def _():
        swapped[...] = left[0, 0, :BLOCK]

    @pl.loop(0, STEPS)
    def _(step):
        row_ = jnp.where(step == 0, yl, yh) * 8 + z
        block_ = jnp.where(step == 0, yh, yl) * 8 + core * 4 + x
        far_copy(step).start()
        sib_left(step, 0).start()
        for stage in range(1, 4):
            for slot, half in order(stage):
                ring_copy(step, slot, half).wait_recv()
                if stage < 3 or (slot == 3) == (half == 0):
                    ring_copy(step, slot + 1 if slot < 4 else slot - 1, half).start()

                @pl.when(user(z, slot) != core)
                def _():
                    sib_copy(step, slot, half).start()
            if stage == 1:
                far_copy(step).wait_recv()
                sib_left(step, 1).start()
                sib_left(step, 0).wait_recv()

                @pl.when(user(z, 0) == core)
                def _():
                    multiply_part(step, 0, 0)

                for slot in (1, 7):
                    @pl.when(user(z, slot) == core)
                    def _():
                        for half in range(2):
                            sib_copy(step, slot, half).wait_recv()
                        multiply_part(step, slot, 0)

                sib_left(step, 1).wait_recv()
                for slot in (0, 1, 7):
                    @pl.when(user(z, slot) == core)
                    def _():
                        multiply_part(step, slot, 1)
            else:
                for slot in (stage, 8 - stage):
                    @pl.when(user(z, slot) == core)
                    def _():
                        for half in range(2):
                            sib_copy(step, slot, half).wait_recv()
                        multiply(step, slot)

        @pl.when(user(z, 4) == core)
        def _():
            for lane in range(2):
                for half in range(2):
                    ring_arrival(step, lane, 4, half).wait_recv()
            multiply(step, 4)

        @pl.when(jnp.logical_and(step == 0, yh != yl))
        def _():
            swap.wait_recv()

        mine = lax.rem(x - z + 8, 4)
        for half in range(2):
            total = outgoing[step, mine, 0, rows(half)].astype(jnp.float32)
            for slot in range(1, 8):
                here = incoming.at[step, slot, rows(half)]
                remote(
                    here, here, sum_send.at[step, 0, 0, half], sum_recv.at[step, slot, half], sibling
                ).wait_recv()
                total += incoming[step, slot, rows(half)].astype(jnp.float32)
            square = select_block(square_ref[row_, block_], total)

            @pl.when(step == 0)
            def _():
                following = 2.0 * swapped[rows(half)].astype(jnp.float32) - square
                left[1, 0, rows(half)] = following.astype(jnp.bfloat16)
                for slot in (1, 7):
                    ring_copy(1, slot, half).start()

            @pl.when(step != 0)
            def _():
                out_ref[rows(half)] = square.astype(jnp.bfloat16)

    @pl.loop(0, STEPS)
    def _(step):
        for slot in range(1, 8):
            for half in range(2):
                ring_copy(step, slot, half).wait_send()
                if slot != 4:
                    @pl.when(user(z, slot) != core)
                    def _():
                        sib_copy(step, slot, half).wait_send()
        far_copy(step).wait_send()
        for part in range(2):
            sib_left(step, part).wait_send()
        for pair in range(4):
            for half in range(2):
                sum_copy(step, pair, 1, half).wait_send()

                @pl.when(elsewhere(pair))
                def _():
                    sum_copy(step, pair, 0, half).wait_send()

    @pl.when(yh != yl)
    def _():
        swap.wait_send()


def local(density, pattern_start, pattern_square):
    block = (BLOCK, BLOCK)
    kind = jnp.bfloat16
    dma = pltpu.SemaphoreType.DMA
    return pl.pallas_call(
        kernel,
        name="purify",
        out_shape=jax.ShapeDtypeStruct(block, kind),
        in_specs=[pl.BlockSpec(memory_space=pl.ANY)] * 3,
        out_specs=pl.BlockSpec(memory_space=pltpu.VMEM),
        scratch_shapes=[
            pltpu.VMEM(block, kind),
            pltpu.SMEM(pattern_start.shape, jnp.int32),
            pltpu.SMEM(pattern_square.shape, jnp.int32),
            dma((3,)),
            pltpu.VMEM((STEPS, 2, 2 * BLOCK, BLOCK), kind),
            pltpu.VMEM((STEPS, 2, 8) + block, kind),
            pltpu.VMEM((STEPS, 4, 2) + block, kind),
            pltpu.VMEM((STEPS, 8) + block, kind),
            pltpu.VMEM(block, kind),
            dma((STEPS, 8, 2)), dma((STEPS, 2, 8, 2)),
            dma((STEPS, 8, 2)), dma((STEPS, 8, 2)),
            dma((STEPS,)), dma((STEPS,)),
            dma((STEPS, 4, 2, 2)), dma((STEPS, 8, 2)),
            dma(()), dma(()),
        ],
        compiler_params=pltpu.CompilerParams(
            collective_id=0, has_side_effects=True, vmem_limit_bytes=62 * 2**20
        ),
    )(pattern_start, pattern_square, density)


def solution(mesh):
    return jax.shard_map(
        local,
        mesh=mesh,
        in_specs=(P("row", ("col", "ka")), P(), P()),
        out_specs=P("row", ("col", "ka")),
        check_vma=False,
    )
```

```python
import jax
import jax.numpy as jnp
from jax import lax
from jax.experimental import pallas as pl
from jax.experimental.pallas import tpu as pltpu
from jax.sharding import PartitionSpec as P

BLOCK = 256
HALF = BLOCK // 2
STEPS = 2
MESH = pl.DeviceIdType.MESH


def select_block(flag, values):
    kept = jnp.full(values.shape, flag, jnp.int32) == 1
    return jnp.where(kept, values, jnp.zeros_like(values))


def order(stage):
    if stage == 4:
        return ((4, 0), (4, 1))
    return ((stage, 0), (8 - stage, 1), (stage, 1), (8 - stage, 0))


def kernel(
    start_hbm, square_hbm, density_hbm, out_ref,
    density_ref, start_ref, square_ref, load_sem, left, right, outgoing, incoming, swapped,
    z_send, z_recv, sib_send, sib_recv, far_send, far_recv, sum_send, sum_recv, swap_send, swap_recv, ready, out_sem, out_block,
):
    row, col, x = lax.axis_index("row"), lax.axis_index("col"), lax.axis_index("ka")
    yh, z = row // 8, lax.rem(row, 8)
    yl, core = col // 2, lax.rem(col, 2)

    def device(yh_, yl_, z_, core_, x_):
        return (yh_ * 8 + z_, yl_ * 2 + core_, x_)

    above, below = lax.rem(z + 1, 8), lax.rem(z + 7, 8)
    sibling = device(yh, yl, z, 1 - core, x)
    across = device(yl, yh, z, core, x)

    def over_yh(step):
        return yh + (1 - step) * (1 - 2 * yh)

    def over_yl(step):
        return yl + step * (1 - 2 * yl)

    loads = [
        pltpu.make_async_copy(src, dst, load_sem.at[i])
        for i, (src, dst) in enumerate(
            ((density_hbm, density_ref), (start_hbm, start_ref), (square_hbm, square_ref))
        )
    ]
    for load in loads:
        load.start()

    barrier = pltpu.get_barrier_semaphore()
    partners = [sibling, device(1 - yh, 1 - yl, z, core, x)]
    for z_ in (above, below):
        partners += [device(yh, yl, z_, core, x), device(yh, yl, z_, 1 - core, x)]
    beside = (device(yh, 1 - yl, z, core, x), device(1 - yh, yl, z, core, x))
    partners += beside
    for dx in (1, 2, 3):
        partners.append(device(yh, yl, z, core, lax.rem(x + dx, 4)))
    for dx in (1, 3):
        partners.append(device(yh, 1 - yl, z, core, lax.rem(x + dx, 4)))
    for partner in partners:
        pl.semaphore_signal(barrier, inc=1, device_id=partner, device_id_type=MESH)

    for load in loads:
        load.wait()
    left[0, 0, :BLOCK] = select_block(start_ref[row, col * 4 + x], density_ref[...])
    pl.semaphore_wait(barrier, len(partners))
    for neighbour in beside:
        pl.semaphore_signal(ready, inc=1, device_id=neighbour, device_id_type=MESH)

    def remote(src, dst, send, recv, target):
        return pltpu.make_async_remote_copy(
            src_ref=src, dst_ref=dst, send_sem=send, recv_sem=recv,
            device_id=target, device_id_type=MESH,
        )

    def user(z_, slot):
        return lax.rem(z_ + slot, 8) // 4

    def rows(half):
        return pl.ds(half * HALF, HALF)

    def ring_copy(step, slot, half):
        downward = slot < 4 or (slot == 4 and half == 0)
        origin = slot - 1 if downward else (slot + 1) % 8
        z_ = below if downward else above
        core_ = user(z_, 4) if slot == 4 else core
        lane = jnp.where(core_ == core, 0, 1) if slot == 4 else 0
        src = left.at[step, 0, rows(half)] if origin == 0 else right.at[step, 0, origin, rows(half)]
        return remote(
            src, right.at[step, lane, slot, rows(half)],
            z_send.at[step, slot, half], z_recv.at[step, lane, slot, half],
            device(yh, yl, z_, core_, x),
        )

    def ring_arrival(step, lane, slot, half):
        here = right.at[step, lane, slot, rows(half)]
        return remote(here, here, z_send.at[step, slot, half], z_recv.at[step, lane, slot, half], sibling)

    def sib_copy(step, slot, half):
        return remote(
            right.at[step, 0, slot, rows(half)], right.at[step, 1, slot, rows(half)],
            sib_send.at[step, slot, half], sib_recv.at[step, slot, half], sibling,
        )

    def sib_left(step, part):
        here = pl.ds(part * BLOCK, BLOCK)
        return remote(
            left.at[step, 0, here], left.at[step, 1, here],
            sib_send.at[step, 0, part], sib_recv.at[step, 0, part], sibling,
        )

    def far_copy(step):
        return remote(
            left.at[step, 0, pl.ds(0, BLOCK)], left.at[step, 0, pl.ds(BLOCK, BLOCK)],
            far_send.at[step], far_recv.at[step],
            device(over_yh(step), over_yl(step), z, core, x),
        )

    swap = remote(left.at[0, 0, pl.ds(0, BLOCK)], swapped, swap_send, swap_recv, across)

    def sum_copy(step, pair, crossing, half):
        x_ = lax.rem(z + pair, 4)
        slot = 4 * crossing + lax.rem(x - x_ + 4, 4)
        target = device(
            jnp.where(crossing != 0, over_yh(1 - step), yh),
            jnp.where(crossing != 0, over_yl(1 - step), yl), z, core, x_,
        )
        return remote(
            outgoing.at[step, pair, crossing, rows(half)], incoming.at[step, slot, rows(half)],
            sum_send.at[step, pair, crossing, half], sum_recv.at[step, slot, half], target,
        )

    def out_copy(half):
        return pltpu.make_async_copy(out_block.at[rows(half)], out_ref.at[rows(half)], out_sem.at[half])

    def elsewhere(pair):
        return lax.rem(z + pair, 4) != x

    def multiply_part(step, slot, part):
        pair = slot % 4
        crossing = jnp.where(yh == yl, part, 1 - part)
        dims = (((1,), (1,)), ((), ()))
        here = pl.ds(part * BLOCK, BLOCK)
        product = jnp.zeros((BLOCK, BLOCK), jnp.float32)
        for lane in range(2):
            other = right[step, lane, slot] if slot else left[step, lane, :BLOCK]
            product += lax.dot_general(
                left[step, lane, here], other, dims, preferred_element_type=jnp.float32
            )
        outgoing[step, pair, crossing] = product.astype(jnp.bfloat16)

        @pl.when(jnp.logical_or(crossing != 0, elsewhere(pair)))
        def _():
            for half in range(2):
                sum_copy(step, pair, crossing, half).start()

    def multiply(step, slot):
        @pl.when(yh == yl)
        def _():
            for part in (1, 0):
                multiply_part(step, slot, part)

        @pl.when(yh != yl)
        def _():
            for part in (0, 1):
                multiply_part(step, slot, part)

    for slot, half in order(1):
        ring_copy(0, slot, half).start()

    @pl.when(yh != yl)
    def _():
        swap.start()

    @pl.when(yh == yl)
    def _():
        swapped[...] = left[0, 0, :BLOCK]

    @pl.loop(0, STEPS)
    def _(step):
        row_ = jnp.where(step == 0, yl, yh) * 8 + z
        block_ = jnp.where(step == 0, yh, yl) * 8 + core * 4 + x
        far_copy(step).start()
        sib_left(step, 0).start()
        for stage in range(1, 4):
            for slot, half in order(stage):
                ring_copy(step, slot, half).wait_recv()
                if stage < 3 or (slot == 3) == (half == 0):
                    ring_copy(step, slot + 1 if slot < 4 else slot - 1, half).start()

                @pl.when(user(z, slot) != core)
                def _():
                    sib_copy(step, slot, half).start()
            if stage == 1:
                far_copy(step).wait_recv()
                sib_left(step, 1).start()
                sib_left(step, 0).wait_recv()

                @pl.when(step == 0)
                def _():
                    pl.semaphore_wait(ready, len(beside))

                @pl.when(user(z, 0) == core)
                def _():
                    multiply_part(step, 0, 0)

                for slot in (1, 7):
                    @pl.when(user(z, slot) == core)
                    def _():
                        for half in range(2):
                            sib_copy(step, slot, half).wait_recv()
                        multiply_part(step, slot, 0)

                sib_left(step, 1).wait_recv()
                for slot in (0, 1, 7):
                    @pl.when(user(z, slot) == core)
                    def _():
                        multiply_part(step, slot, 1)
            else:
                for slot in (stage, 8 - stage):
                    @pl.when(user(z, slot) == core)
                    def _():
                        for half in range(2):
                            sib_copy(step, slot, half).wait_recv()
                        multiply(step, slot)

        @pl.when(user(z, 4) == core)
        def _():
            for lane in range(2):
                for half in range(2):
                    ring_arrival(step, lane, 4, half).wait_recv()
            multiply(step, 4)

        @pl.when(jnp.logical_and(step == 0, yh != yl))
        def _():
            swap.wait_recv()

        mine = lax.rem(x - z + 8, 4)
        for half in range(2):
            total = outgoing[step, mine, 0, rows(half)].astype(jnp.float32)
            for slot in range(1, 8):
                here = incoming.at[step, slot, rows(half)]
                remote(
                    here, here, sum_send.at[step, 0, 0, half], sum_recv.at[step, slot, half], sibling
                ).wait_recv()
                total += incoming[step, slot, rows(half)].astype(jnp.float32)
            square = select_block(square_ref[row_, block_], total)

            @pl.when(step == 0)
            def _():
                following = 2.0 * swapped[rows(half)].astype(jnp.float32) - square
                left[1, 0, rows(half)] = following.astype(jnp.bfloat16)
                for slot in (1, 7):
                    ring_copy(1, slot, half).start()

            @pl.when(step != 0)
            def _():
                out_block[rows(half)] = square.astype(jnp.bfloat16)
                out_copy(half).start()

    @pl.loop(0, STEPS)
    def _(step):
        for slot in range(1, 8):
            for half in range(2):
                ring_copy(step, slot, half).wait_send()
                if slot != 4:
                    @pl.when(user(z, slot) != core)
                    def _():
                        sib_copy(step, slot, half).wait_send()
        far_copy(step).wait_send()
        for part in range(2):
            sib_left(step, part).wait_send()
        for pair in range(4):
            for half in range(2):
                sum_copy(step, pair, 1, half).wait_send()

                @pl.when(elsewhere(pair))
                def _():
                    sum_copy(step, pair, 0, half).wait_send()

    @pl.when(yh != yl)
    def _():
        swap.wait_send()

    for half in range(2):
        out_copy(half).wait()


def local(density, pattern_start, pattern_square):
    block = (BLOCK, BLOCK)
    kind = jnp.bfloat16
    dma = pltpu.SemaphoreType.DMA
    return pl.pallas_call(
        kernel,
        name="purify",
        out_shape=jax.ShapeDtypeStruct(block, kind),
        in_specs=[pl.BlockSpec(memory_space=pl.ANY)] * 3,
        out_specs=pl.BlockSpec(memory_space=pl.ANY),
        scratch_shapes=[
            pltpu.VMEM(block, kind),
            pltpu.SMEM(pattern_start.shape, jnp.int32),
            pltpu.SMEM(pattern_square.shape, jnp.int32),
            dma((3,)),
            pltpu.VMEM((STEPS, 2, 2 * BLOCK, BLOCK), kind),
            pltpu.VMEM((STEPS, 2, 8) + block, kind),
            pltpu.VMEM((STEPS, 4, 2) + block, kind),
            pltpu.VMEM((STEPS, 8) + block, kind),
            pltpu.VMEM(block, kind),
            dma((STEPS, 8, 2)), dma((STEPS, 2, 8, 2)),
            dma((STEPS, 8, 2)), dma((STEPS, 8, 2)),
            dma((STEPS,)), dma((STEPS,)),
            dma((STEPS, 4, 2, 2)), dma((STEPS, 8, 2)),
            dma(()), dma(()),
            pltpu.SemaphoreType.REGULAR, dma((2,)), pltpu.VMEM(block, kind),
        ],
        compiler_params=pltpu.CompilerParams(
            collective_id=0, has_side_effects=True, vmem_limit_bytes=62 * 2**20
        ),
    )(pattern_start, pattern_square, density)


def solution(mesh):
    return jax.shard_map(
        local,
        mesh=mesh,
        in_specs=(P("row", ("col", "ka")), P(), P()),
        out_specs=P("row", ("col", "ka")),
        check_vma=False,
    )
```

```python
import jax
import jax.numpy as jnp
from jax import lax
from jax.experimental import pallas as pl
from jax.experimental.pallas import tpu as pltpu
from jax.sharding import PartitionSpec as P

BLOCK = 256
HALF = BLOCK // 2
STEPS = 2
MESH = pl.DeviceIdType.MESH


def select_block(flag, values):
    kept = jnp.full(values.shape, flag, jnp.int32) == 1
    return jnp.where(kept, values, jnp.zeros_like(values))


def order(stage):
    if stage == 4:
        return ((4, 0), (4, 1))
    return ((stage, 0), (8 - stage, 1), (stage, 1), (8 - stage, 0))


def kernel(
    start_hbm, square_hbm, density_hbm, out_ref,
    density_ref, start_ref, square_ref, load_sem, left, right, outgoing, incoming, swapped,
    z_send, z_recv, sib_send, sib_recv, far_send, far_recv, sum_send, sum_recv, swap_send, swap_recv, ready, out_sem, out_block,
):
    row, col, x = lax.axis_index("row"), lax.axis_index("col"), lax.axis_index("ka")
    yh, z = row // 8, lax.rem(row, 8)
    yl, core = col // 2, lax.rem(col, 2)

    def device(yh_, yl_, z_, core_, x_):
        return (yh_ * 8 + z_, yl_ * 2 + core_, x_)

    above, below = lax.rem(z + 1, 8), lax.rem(z + 7, 8)
    sibling = device(yh, yl, z, 1 - core, x)
    across = device(yl, yh, z, core, x)

    def over_yh(step):
        return yh + (1 - step) * (1 - 2 * yh)

    def over_yl(step):
        return yl + step * (1 - 2 * yl)

    loads = [
        pltpu.make_async_copy(src, dst, load_sem.at[i])
        for i, (src, dst) in enumerate(
            ((density_hbm, density_ref), (start_hbm, start_ref), (square_hbm, square_ref))
        )
    ]
    for load in loads:
        load.start()

    barrier = pltpu.get_barrier_semaphore()
    partners = [sibling, device(1 - yh, 1 - yl, z, core, x)]
    for z_ in (above, below):
        partners += [device(yh, yl, z_, core, x), device(yh, yl, z_, 1 - core, x)]
    beside = (device(yh, 1 - yl, z, core, x), device(1 - yh, yl, z, core, x))
    partners += beside
    for dx in (1, 2, 3):
        partners.append(device(yh, yl, z, core, lax.rem(x + dx, 4)))
    for dx in (1, 3):
        partners.append(device(yh, 1 - yl, z, core, lax.rem(x + dx, 4)))
    for partner in partners:
        pl.semaphore_signal(barrier, inc=1, device_id=partner, device_id_type=MESH)

    for load in loads[:2]:
        load.wait()
    left[0, 0, :BLOCK] = select_block(start_ref[row, col * 4 + x], density_ref[...])
    pl.semaphore_wait(barrier, len(partners))

    def remote(src, dst, send, recv, target):
        return pltpu.make_async_remote_copy(
            src_ref=src, dst_ref=dst, send_sem=send, recv_sem=recv,
            device_id=target, device_id_type=MESH,
        )

    def user(z_, slot):
        return lax.rem(z_ + slot, 8) // 4

    def rows(half):
        return pl.ds(half * HALF, HALF)

    def ring_copy(step, slot, half):
        downward = slot < 4 or (slot == 4 and half == 0)
        origin = slot - 1 if downward else (slot + 1) % 8
        z_ = below if downward else above
        core_ = user(z_, 4) if slot == 4 else core
        lane = jnp.where(core_ == core, 0, 1) if slot == 4 else 0
        src = left.at[step, 0, rows(half)] if origin == 0 else right.at[step, 0, origin, rows(half)]
        return remote(
            src, right.at[step, lane, slot, rows(half)],
            z_send.at[step, slot, half], z_recv.at[step, lane, slot, half],
            device(yh, yl, z_, core_, x),
        )

    def ring_arrival(step, lane, slot, half):
        here = right.at[step, lane, slot, rows(half)]
        return remote(here, here, z_send.at[step, slot, half], z_recv.at[step, lane, slot, half], sibling)

    def sib_copy(step, slot):
        return remote(
            right.at[step, 0, slot], right.at[step, 1, slot],
            sib_send.at[step, slot, 0], sib_recv.at[step, slot, 0], sibling,
        )

    def sib_left(step, part):
        here = pl.ds(part * BLOCK, BLOCK)
        return remote(
            left.at[step, 0, here], left.at[step, 1, here],
            sib_send.at[step, 0, part], sib_recv.at[step, 0, part], sibling,
        )

    def far_copy(step):
        return remote(
            left.at[step, 0, pl.ds(0, BLOCK)], left.at[step, 0, pl.ds(BLOCK, BLOCK)],
            far_send.at[step], far_recv.at[step],
            device(over_yh(step), over_yl(step), z, core, x),
        )

    swap = remote(left.at[0, 0, pl.ds(0, BLOCK)], swapped, swap_send, swap_recv, across)

    def sum_copy(step, pair, crossing, half):
        x_ = lax.rem(z + pair, 4)
        slot = 4 * crossing + lax.rem(x - x_ + 4, 4)
        target = device(
            jnp.where(crossing != 0, over_yh(1 - step), yh),
            jnp.where(crossing != 0, over_yl(1 - step), yl), z, core, x_,
        )
        return remote(
            outgoing.at[step, pair, crossing, rows(half)], incoming.at[step, slot, rows(half)],
            sum_send.at[step, pair, crossing, half], sum_recv.at[step, slot, half], target,
        )

    def out_copy(half):
        return pltpu.make_async_copy(out_block.at[rows(half)], out_ref.at[rows(half)], out_sem.at[half])

    def elsewhere(pair):
        return lax.rem(z + pair, 4) != x

    def multiply_part(step, slot, part):
        pair = slot % 4
        crossing = jnp.where(yh == yl, part, 1 - part)
        dims = (((1,), (1,)), ((), ()))
        here = pl.ds(part * BLOCK, BLOCK)
        product = jnp.zeros((BLOCK, BLOCK), jnp.float32)
        for lane in range(2):
            other = right[step, lane, slot] if slot else left[step, lane, :BLOCK]
            product += lax.dot_general(
                left[step, lane, here], other, dims, preferred_element_type=jnp.float32
            )
        outgoing[step, pair, crossing] = product.astype(jnp.bfloat16)

        @pl.when(jnp.logical_or(crossing != 0, elsewhere(pair)))
        def _():
            for half in range(2):
                sum_copy(step, pair, crossing, half).start()

    def multiply(step, slot):
        @pl.when(yh == yl)
        def _():
            for part in (1, 0):
                multiply_part(step, slot, part)

        @pl.when(yh != yl)
        def _():
            for part in (0, 1):
                multiply_part(step, slot, part)

    for slot, half in order(1):
        ring_copy(0, slot, half).start()
    for neighbour in beside:
        pl.semaphore_signal(ready, inc=1, device_id=neighbour, device_id_type=MESH)
    loads[2].wait()

    @pl.when(yh != yl)
    def _():
        swap.start()

    @pl.when(yh == yl)
    def _():
        swapped[...] = left[0, 0, :BLOCK]

    @pl.loop(0, STEPS)
    def _(step):
        row_ = jnp.where(step == 0, yl, yh) * 8 + z
        block_ = jnp.where(step == 0, yh, yl) * 8 + core * 4 + x
        far_copy(step).start()
        sib_left(step, 0).start()
        for stage in range(1, 4):
            for slot, half in order(stage):
                ring_copy(step, slot, half).wait_recv()
                if stage < 3 or (slot == 3) == (half == 0):
                    ring_copy(step, slot + 1 if slot < 4 else slot - 1, half).start()

                if (slot < 4) == (half == 1):
                    @pl.when(user(z, slot) != core)
                    def _():
                        sib_copy(step, slot).start()
            if stage == 1:
                far_copy(step).wait_recv()
                sib_left(step, 1).start()
                sib_left(step, 0).wait_recv()

                @pl.when(step == 0)
                def _():
                    pl.semaphore_wait(ready, len(beside))

                @pl.when(user(z, 0) == core)
                def _():
                    multiply_part(step, 0, 0)

                for slot in (1, 7):
                    @pl.when(user(z, slot) == core)
                    def _():
                        sib_copy(step, slot).wait_recv()
                        multiply_part(step, slot, 0)

                sib_left(step, 1).wait_recv()
                for slot in (0, 1, 7):
                    @pl.when(user(z, slot) == core)
                    def _():
                        multiply_part(step, slot, 1)
            else:
                for slot in (stage, 8 - stage):
                    @pl.when(user(z, slot) == core)
                    def _():
                        sib_copy(step, slot).wait_recv()
                        multiply(step, slot)

        @pl.when(user(z, 4) == core)
        def _():
            for lane in range(2):
                for half in range(2):
                    ring_arrival(step, lane, 4, half).wait_recv()
            multiply(step, 4)

        @pl.when(jnp.logical_and(step == 0, yh != yl))
        def _():
            swap.wait_recv()

        mine = lax.rem(x - z + 8, 4)
        for half in range(2):
            total = outgoing[step, mine, 0, rows(half)].astype(jnp.float32)
            for slot in range(1, 8):
                here = incoming.at[step, slot, rows(half)]
                remote(
                    here, here, sum_send.at[step, 0, 0, half], sum_recv.at[step, slot, half], sibling
                ).wait_recv()
                total += incoming[step, slot, rows(half)].astype(jnp.float32)
            square = select_block(square_ref[row_, block_], total)

            @pl.when(step == 0)
            def _():
                following = 2.0 * swapped[rows(half)].astype(jnp.float32) - square
                left[1, 0, rows(half)] = following.astype(jnp.bfloat16)
                for slot in (1, 7):
                    ring_copy(1, slot, half).start()

            @pl.when(step != 0)
            def _():
                out_block[rows(half)] = square.astype(jnp.bfloat16)
                out_copy(half).start()

    @pl.loop(0, STEPS)
    def _(step):
        for slot in range(1, 8):
            for half in range(2):
                ring_copy(step, slot, half).wait_send()
                if slot != 4 and half == 0:
                    @pl.when(user(z, slot) != core)
                    def _():
                        sib_copy(step, slot).wait_send()
        far_copy(step).wait_send()
        for part in range(2):
            sib_left(step, part).wait_send()
        for pair in range(4):
            for half in range(2):
                sum_copy(step, pair, 1, half).wait_send()

                @pl.when(elsewhere(pair))
                def _():
                    sum_copy(step, pair, 0, half).wait_send()

    @pl.when(yh != yl)
    def _():
        swap.wait_send()

    for half in range(2):
        out_copy(half).wait()


def local(density, pattern_start, pattern_square):
    block = (BLOCK, BLOCK)
    kind = jnp.bfloat16
    dma = pltpu.SemaphoreType.DMA
    return pl.pallas_call(
        kernel,
        name="purify",
        out_shape=jax.ShapeDtypeStruct(block, kind),
        in_specs=[pl.BlockSpec(memory_space=pl.ANY)] * 3,
        out_specs=pl.BlockSpec(memory_space=pl.ANY),
        scratch_shapes=[
            pltpu.VMEM(block, kind),
            pltpu.SMEM(pattern_start.shape, jnp.int32),
            pltpu.SMEM(pattern_square.shape, jnp.int32),
            dma((3,)),
            pltpu.VMEM((STEPS, 2, 2 * BLOCK, BLOCK), kind),
            pltpu.VMEM((STEPS, 2, 8) + block, kind),
            pltpu.VMEM((STEPS, 4, 2) + block, kind),
            pltpu.VMEM((STEPS, 8) + block, kind),
            pltpu.VMEM(block, kind),
            dma((STEPS, 8, 2)), dma((STEPS, 2, 8, 2)),
            dma((STEPS, 8, 2)), dma((STEPS, 8, 2)),
            dma((STEPS,)), dma((STEPS,)),
            dma((STEPS, 4, 2, 2)), dma((STEPS, 8, 2)),
            dma(()), dma(()),
            pltpu.SemaphoreType.REGULAR, dma((2,)), pltpu.VMEM(block, kind),
        ],
        compiler_params=pltpu.CompilerParams(
            collective_id=0, has_side_effects=True, vmem_limit_bytes=62 * 2**20
        ),
    )(pattern_start, pattern_square, density)


def solution(mesh):
    return jax.shard_map(
        local,
        mesh=mesh,
        in_specs=(P("row", ("col", "ka")), P(), P()),
        out_specs=P("row", ("col", "ka")),
        check_vma=False,
    )
```

```python
import jax
import jax.numpy as jnp
from jax import lax
from jax.experimental import pallas as pl
from jax.experimental.pallas import tpu as pltpu
from jax.sharding import PartitionSpec as P

BLOCK = 256
HALF = BLOCK // 2
STEPS = 2
MESH = pl.DeviceIdType.MESH


def select_block(flag, values):
    kept = jnp.full(values.shape, flag, jnp.int32) == 1
    return jnp.where(kept, values, jnp.zeros_like(values))


def order(stage):
    if stage == 4:
        return ((4, 0), (4, 1))
    return ((stage, 0), (8 - stage, 1), (stage, 1), (8 - stage, 0))


def last(slot, half):
    return slot == 4 or (slot, half) in ((3, 1), (5, 0))


def kernel(
    start_hbm, square_hbm, density_hbm, out_ref,
    density_ref, start_ref, square_ref, load_sem, left, right, outgoing, incoming, swapped,
    z_send, z_recv, sib_send, sib_recv, far_send, far_recv, sum_send, sum_recv, swap_send, swap_recv, ready, out_sem, out_block,
):
    row, col, x = lax.axis_index("row"), lax.axis_index("col"), lax.axis_index("ka")
    yh, z = row // 8, lax.rem(row, 8)
    yl, core = col // 2, lax.rem(col, 2)

    def device(yh_, yl_, z_, core_, x_):
        return (yh_ * 8 + z_, yl_ * 2 + core_, x_)

    above, below = lax.rem(z + 1, 8), lax.rem(z + 7, 8)
    sibling = device(yh, yl, z, 1 - core, x)
    across = device(yl, yh, z, core, x)

    def over_yh(step):
        return yh + (1 - step) * (1 - 2 * yh)

    def over_yl(step):
        return yl + step * (1 - 2 * yl)

    loads = [
        pltpu.make_async_copy(src, dst, load_sem.at[i])
        for i, (src, dst) in enumerate(
            ((density_hbm, density_ref), (start_hbm, start_ref), (square_hbm, square_ref))
        )
    ]
    for load in loads:
        load.start()

    barrier = pltpu.get_barrier_semaphore()
    partners = [sibling, device(1 - yh, 1 - yl, z, core, x)]
    for z_ in (above, below):
        partners += [device(yh, yl, z_, core, x), device(yh, yl, z_, 1 - core, x)]
    beside = (device(yh, 1 - yl, z, core, x), device(1 - yh, yl, z, core, x))
    partners += beside
    for dx in (1, 2, 3):
        partners.append(device(yh, yl, z, core, lax.rem(x + dx, 4)))
    for dx in (1, 3):
        partners.append(device(yh, 1 - yl, z, core, lax.rem(x + dx, 4)))
    for partner in partners:
        pl.semaphore_signal(barrier, inc=1, device_id=partner, device_id_type=MESH)

    for load in loads:
        load.wait()
    left[0, 0, :BLOCK] = select_block(start_ref[row, col * 4 + x], density_ref[...])
    pl.semaphore_wait(barrier, len(partners))
    for neighbour in beside:
        pl.semaphore_signal(ready, inc=1, device_id=neighbour, device_id_type=MESH)

    def remote(src, dst, send, recv, target):
        return pltpu.make_async_remote_copy(
            src_ref=src, dst_ref=dst, send_sem=send, recv_sem=recv,
            device_id=target, device_id_type=MESH,
        )

    def user(z_, slot):
        return lax.rem(z_ + slot, 8) // 4

    def rows(half):
        return pl.ds(half * HALF, HALF)

    def ring_copy(step, slot, half):
        downward = slot < 4 or (slot == 4 and half == 0)
        origin = slot - 1 if downward else (slot + 1) % 8
        z_ = below if downward else above
        core_ = user(z_, slot) if last(slot, half) else core
        lane = jnp.where(core_ == core, 0, 1) if last(slot, half) else 0
        src = left.at[step, 0, rows(half)] if origin == 0 else right.at[step, 0, origin, rows(half)]
        return remote(
            src, right.at[step, lane, slot, rows(half)],
            z_send.at[step, slot, half], z_recv.at[step, lane, slot, half],
            device(yh, yl, z_, core_, x),
        )

    def ring_arrival(step, lane, slot, half):
        here = right.at[step, lane, slot, rows(half)]
        return remote(here, here, z_send.at[step, slot, half], z_recv.at[step, lane, slot, half], sibling)

    def sib_copy(step, slot, half):
        return remote(
            right.at[step, 0, slot, rows(half)], right.at[step, 1, slot, rows(half)],
            sib_send.at[step, slot, half], sib_recv.at[step, slot, half], sibling,
        )

    def sib_left(step, part):
        here = pl.ds(part * BLOCK, BLOCK)
        return remote(
            left.at[step, 0, here], left.at[step, 1, here],
            sib_send.at[step, 0, part], sib_recv.at[step, 0, part], sibling,
        )

    def far_copy(step):
        return remote(
            left.at[step, 0, pl.ds(0, BLOCK)], left.at[step, 0, pl.ds(BLOCK, BLOCK)],
            far_send.at[step], far_recv.at[step],
            device(over_yh(step), over_yl(step), z, core, x),
        )

    swap = remote(left.at[0, 0, pl.ds(0, BLOCK)], swapped, swap_send, swap_recv, across)

    def sum_copy(step, pair, crossing, half):
        x_ = lax.rem(z + pair, 4)
        slot = 4 * crossing + lax.rem(x - x_ + 4, 4)
        target = device(
            jnp.where(crossing != 0, over_yh(1 - step), yh),
            jnp.where(crossing != 0, over_yl(1 - step), yl), z, core, x_,
        )
        return remote(
            outgoing.at[step, pair, crossing, rows(half)], incoming.at[step, slot, rows(half)],
            sum_send.at[step, pair, crossing, half], sum_recv.at[step, slot, half], target,
        )

    def out_copy(half):
        return pltpu.make_async_copy(out_block.at[rows(half)], out_ref.at[rows(half)], out_sem.at[half])

    def elsewhere(pair):
        return lax.rem(z + pair, 4) != x

    def multiply_part(step, slot, part):
        pair = slot % 4
        crossing = jnp.where(yh == yl, part, 1 - part)
        dims = (((1,), (1,)), ((), ()))
        here = pl.ds(part * BLOCK, BLOCK)
        product = jnp.zeros((BLOCK, BLOCK), jnp.float32)
        for lane in range(2):
            other = right[step, lane, slot] if slot else left[step, lane, :BLOCK]
            product += lax.dot_general(
                left[step, lane, here], other, dims, preferred_element_type=jnp.float32
            )
        outgoing[step, pair, crossing] = product.astype(jnp.bfloat16)

        @pl.when(jnp.logical_or(crossing != 0, elsewhere(pair)))
        def _():
            for half in range(2):
                sum_copy(step, pair, crossing, half).start()

    def multiply(step, slot):
        @pl.when(yh == yl)
        def _():
            for part in (1, 0):
                multiply_part(step, slot, part)

        @pl.when(yh != yl)
        def _():
            for part in (0, 1):
                multiply_part(step, slot, part)

    for slot, half in order(1):
        ring_copy(0, slot, half).start()

    @pl.when(yh != yl)
    def _():
        swap.start()

    @pl.when(yh == yl)
    def _():
        swapped[...] = left[0, 0, :BLOCK]

    @pl.loop(0, STEPS)
    def _(step):
        row_ = jnp.where(step == 0, yl, yh) * 8 + z
        block_ = jnp.where(step == 0, yh, yl) * 8 + core * 4 + x
        far_copy(step).start()
        sib_left(step, 0).start()
        for stage in range(1, 4):
            for slot, half in order(stage):
                if last(slot, half):
                    continue
                ring_copy(step, slot, half).wait_recv()
                if stage < 3 or (slot == 3) == (half == 0):
                    ring_copy(step, slot + 1 if slot < 4 else slot - 1, half).start()

                @pl.when(user(z, slot) != core)
                def _():
                    sib_copy(step, slot, half).start()
            if stage == 1:
                far_copy(step).wait_recv()
                sib_left(step, 1).start()
                sib_left(step, 0).wait_recv()

                @pl.when(step == 0)
                def _():
                    pl.semaphore_wait(ready, len(beside))

                @pl.when(user(z, 0) == core)
                def _():
                    multiply_part(step, 0, 0)

                for slot in (1, 7):
                    @pl.when(user(z, slot) == core)
                    def _():
                        for half in range(2):
                            sib_copy(step, slot, half).wait_recv()
                        multiply_part(step, slot, 0)

                sib_left(step, 1).wait_recv()
                for slot in (0, 1, 7):
                    @pl.when(user(z, slot) == core)
                    def _():
                        multiply_part(step, slot, 1)
            else:
                for slot in (stage, 8 - stage):
                    @pl.when(user(z, slot) == core)
                    def _():
                        for half in range(2):
                            if last(slot, half):
                                for lane in range(2):
                                    ring_arrival(step, lane, slot, half).wait_recv()
                            else:
                                sib_copy(step, slot, half).wait_recv()
                        multiply(step, slot)

        @pl.when(user(z, 4) == core)
        def _():
            for lane in range(2):
                for half in range(2):
                    ring_arrival(step, lane, 4, half).wait_recv()
            multiply(step, 4)

        @pl.when(jnp.logical_and(step == 0, yh != yl))
        def _():
            swap.wait_recv()

        mine = lax.rem(x - z + 8, 4)
        for half in range(2):
            total = outgoing[step, mine, 0, rows(half)].astype(jnp.float32)
            for slot in range(1, 8):
                here = incoming.at[step, slot, rows(half)]
                remote(
                    here, here, sum_send.at[step, 0, 0, half], sum_recv.at[step, slot, half], sibling
                ).wait_recv()
                total += incoming[step, slot, rows(half)].astype(jnp.float32)
            square = select_block(square_ref[row_, block_], total)

            @pl.when(step == 0)
            def _():
                following = 2.0 * swapped[rows(half)].astype(jnp.float32) - square
                left[1, 0, rows(half)] = following.astype(jnp.bfloat16)
                for slot in (1, 7):
                    ring_copy(1, slot, half).start()

            @pl.when(step != 0)
            def _():
                out_block[rows(half)] = square.astype(jnp.bfloat16)
                out_copy(half).start()

    @pl.loop(0, STEPS)
    def _(step):
        for slot in range(1, 8):
            for half in range(2):
                ring_copy(step, slot, half).wait_send()
                if not last(slot, half):
                    @pl.when(user(z, slot) != core)
                    def _():
                        sib_copy(step, slot, half).wait_send()
        far_copy(step).wait_send()
        for part in range(2):
            sib_left(step, part).wait_send()
        for pair in range(4):
            for half in range(2):
                sum_copy(step, pair, 1, half).wait_send()

                @pl.when(elsewhere(pair))
                def _():
                    sum_copy(step, pair, 0, half).wait_send()

    @pl.when(yh != yl)
    def _():
        swap.wait_send()

    for half in range(2):
        out_copy(half).wait()


def local(density, pattern_start, pattern_square):
    block = (BLOCK, BLOCK)
    kind = jnp.bfloat16
    dma = pltpu.SemaphoreType.DMA
    return pl.pallas_call(
        kernel,
        name="purify",
        out_shape=jax.ShapeDtypeStruct(block, kind),
        in_specs=[pl.BlockSpec(memory_space=pl.ANY)] * 3,
        out_specs=pl.BlockSpec(memory_space=pl.ANY),
        scratch_shapes=[
            pltpu.VMEM(block, kind),
            pltpu.SMEM(pattern_start.shape, jnp.int32),
            pltpu.SMEM(pattern_square.shape, jnp.int32),
            dma((3,)),
            pltpu.VMEM((STEPS, 2, 2 * BLOCK, BLOCK), kind),
            pltpu.VMEM((STEPS, 2, 8) + block, kind),
            pltpu.VMEM((STEPS, 4, 2) + block, kind),
            pltpu.VMEM((STEPS, 8) + block, kind),
            pltpu.VMEM(block, kind),
            dma((STEPS, 8, 2)), dma((STEPS, 2, 8, 2)),
            dma((STEPS, 8, 2)), dma((STEPS, 8, 2)),
            dma((STEPS,)), dma((STEPS,)),
            dma((STEPS, 4, 2, 2)), dma((STEPS, 8, 2)),
            dma(()), dma(()),
            pltpu.SemaphoreType.REGULAR, dma((2,)), pltpu.VMEM(block, kind),
        ],
        compiler_params=pltpu.CompilerParams(
            collective_id=0, has_side_effects=True, vmem_limit_bytes=62 * 2**20
        ),
    )(pattern_start, pattern_square, density)


def solution(mesh):
    return jax.shard_map(
        local,
        mesh=mesh,
        in_specs=(P("row", ("col", "ka")), P(), P()),
        out_specs=P("row", ("col", "ka")),
        check_vma=False,
    )
```

```python
import jax
import jax.numpy as jnp
from jax import lax
from jax.experimental import pallas as pl
from jax.experimental.pallas import tpu as pltpu
from jax.sharding import PartitionSpec as P

BLOCK = 256
HALF = BLOCK // 2
STEPS = 2
MESH = pl.DeviceIdType.MESH


def select_block(flag, values):
    kept = jnp.full(values.shape, flag, jnp.int32) == 1
    return jnp.where(kept, values, jnp.zeros_like(values))


def order(stage):
    if stage == 4:
        return ((4, 0), (4, 1))
    return ((stage, 0), (8 - stage, 1), (stage, 1), (8 - stage, 0))


def last(slot, half):
    return slot == 4 or (slot, half) in ((3, 1), (5, 0))


def kernel(
    start_hbm, square_hbm, density_hbm, out_ref,
    density_ref, start_ref, square_ref, load_sem, left, right, outgoing, incoming, swapped,
    z_send, z_recv, sib_send, sib_recv, far_send, far_recv, sum_send, sum_recv, swap_send, swap_recv, ready, out_sem, out_block,
):
    row, col, x = lax.axis_index("row"), lax.axis_index("col"), lax.axis_index("ka")
    yh, z = row // 8, lax.rem(row, 8)
    yl, core = col // 2, lax.rem(col, 2)

    def device(yh_, yl_, z_, core_, x_):
        return (yh_ * 8 + z_, yl_ * 2 + core_, x_)

    above, below = lax.rem(z + 1, 8), lax.rem(z + 7, 8)
    sibling = device(yh, yl, z, 1 - core, x)
    across = device(yl, yh, z, core, x)

    def over_yh(step):
        return yh + (1 - step) * (1 - 2 * yh)

    def over_yl(step):
        return yl + step * (1 - 2 * yl)

    loads = [
        pltpu.make_async_copy(src, dst, load_sem.at[i])
        for i, (src, dst) in enumerate(
            ((density_hbm, density_ref), (start_hbm, start_ref), (square_hbm, square_ref))
        )
    ]
    for load in loads:
        load.start()

    barrier = pltpu.get_barrier_semaphore()
    partners = [sibling, device(1 - yh, 1 - yl, z, core, x)]
    for z_ in (above, below):
        partners += [device(yh, yl, z_, core, x), device(yh, yl, z_, 1 - core, x)]
    beside = (device(yh, 1 - yl, z, core, x), device(1 - yh, yl, z, core, x))
    partners += beside
    for dx in (1, 2, 3):
        partners.append(device(yh, yl, z, core, lax.rem(x + dx, 4)))
    for dx in (1, 3):
        partners.append(device(yh, 1 - yl, z, core, lax.rem(x + dx, 4)))
    for partner in partners:
        pl.semaphore_signal(barrier, inc=1, device_id=partner, device_id_type=MESH)

    for load in loads:
        load.wait()
    left[0, 0, :BLOCK] = select_block(start_ref[row, col * 4 + x], density_ref[...])
    pl.semaphore_wait(barrier, len(partners))

    def remote(src, dst, send, recv, target):
        return pltpu.make_async_remote_copy(
            src_ref=src, dst_ref=dst, send_sem=send, recv_sem=recv,
            device_id=target, device_id_type=MESH,
        )

    def user(z_, slot):
        return lax.rem(z_ + slot, 8) // 4

    def rows(half):
        return pl.ds(half * HALF, HALF)

    def ring_copy(step, slot, half):
        downward = slot < 4 or (slot == 4 and half == 0)
        origin = slot - 1 if downward else (slot + 1) % 8
        z_ = below if downward else above
        core_ = user(z_, slot) if last(slot, half) else core
        lane = jnp.where(core_ == core, 0, 1) if last(slot, half) else 0
        src = left.at[step, 0, rows(half)] if origin == 0 else right.at[step, 0, origin, rows(half)]
        return remote(
            src, right.at[step, lane, slot, rows(half)],
            z_send.at[step, slot, half], z_recv.at[step, lane, slot, half],
            device(yh, yl, z_, core_, x),
        )

    def ring_arrival(step, lane, slot, half):
        here = right.at[step, lane, slot, rows(half)]
        return remote(here, here, z_send.at[step, slot, half], z_recv.at[step, lane, slot, half], sibling)

    def sib_copy(step, slot, half):
        return remote(
            right.at[step, 0, slot, rows(half)], right.at[step, 1, slot, rows(half)],
            sib_send.at[step, slot, half], sib_recv.at[step, slot, half], sibling,
        )

    def sib_left(step, part):
        here = pl.ds(part * BLOCK, BLOCK)
        return remote(
            left.at[step, 0, here], left.at[step, 1, here],
            sib_send.at[step, 0, part], sib_recv.at[step, 0, part], sibling,
        )

    def far_copy(step):
        return remote(
            left.at[step, 0, pl.ds(0, BLOCK)], left.at[step, 0, pl.ds(BLOCK, BLOCK)],
            far_send.at[step], far_recv.at[step],
            device(over_yh(step), over_yl(step), z, core, x),
        )

    swap = remote(left.at[0, 0, pl.ds(0, BLOCK)], swapped, swap_send, swap_recv, across)

    def sum_copy(step, pair, crossing, half):
        x_ = lax.rem(z + pair, 4)
        slot = 4 * crossing + lax.rem(x - x_ + 4, 4)
        target = device(
            jnp.where(crossing != 0, over_yh(1 - step), yh),
            jnp.where(crossing != 0, over_yl(1 - step), yl), z, core, x_,
        )
        return remote(
            outgoing.at[step, pair, crossing, rows(half)], incoming.at[step, slot, rows(half)],
            sum_send.at[step, pair, crossing, half], sum_recv.at[step, slot, half], target,
        )

    def out_copy(half):
        return pltpu.make_async_copy(out_block.at[rows(half)], out_ref.at[rows(half)], out_sem.at[half])

    def elsewhere(pair):
        return lax.rem(z + pair, 4) != x

    def multiply_part(step, slot, part):
        pair = slot % 4
        crossing = jnp.where(yh == yl, part, 1 - part)
        dims = (((1,), (1,)), ((), ()))
        here = pl.ds(part * BLOCK, BLOCK)
        product = jnp.zeros((BLOCK, BLOCK), jnp.float32)
        for lane in range(2):
            other = right[step, lane, slot] if slot else left[step, lane, :BLOCK]
            product += lax.dot_general(
                left[step, lane, here], other, dims, preferred_element_type=jnp.float32
            )
        outgoing[step, pair, crossing] = product.astype(jnp.bfloat16)

        @pl.when(jnp.logical_or(crossing != 0, elsewhere(pair)))
        def _():
            for half in range(2):
                sum_copy(step, pair, crossing, half).start()

    def multiply(step, slot):
        @pl.when(yh == yl)
        def _():
            for part in (1, 0):
                multiply_part(step, slot, part)

        @pl.when(yh != yl)
        def _():
            for part in (0, 1):
                multiply_part(step, slot, part)

    for slot, half in order(1):
        ring_copy(0, slot, half).start()
    for neighbour in beside:
        pl.semaphore_signal(ready, inc=1, device_id=neighbour, device_id_type=MESH)

    @pl.when(yh != yl)
    def _():
        swap.start()

    @pl.when(yh == yl)
    def _():
        swapped[...] = left[0, 0, :BLOCK]

    @pl.loop(0, STEPS)
    def _(step):
        row_ = jnp.where(step == 0, yl, yh) * 8 + z
        block_ = jnp.where(step == 0, yh, yl) * 8 + core * 4 + x
        far_copy(step).start()
        sib_left(step, 0).start()
        for stage in range(1, 4):
            for slot, half in order(stage):
                if last(slot, half):
                    continue
                ring_copy(step, slot, half).wait_recv()
                if stage < 3 or (slot == 3) == (half == 0):
                    ring_copy(step, slot + 1 if slot < 4 else slot - 1, half).start()

                @pl.when(user(z, slot) != core)
                def _():
                    sib_copy(step, slot, half).start()
            if stage == 1:
                far_copy(step).wait_recv()
                sib_left(step, 1).start()
                sib_left(step, 0).wait_recv()

                @pl.when(step == 0)
                def _():
                    pl.semaphore_wait(ready, len(beside))

                @pl.when(user(z, 0) == core)
                def _():
                    multiply_part(step, 0, 0)

                for slot in (1, 7):
                    @pl.when(user(z, slot) == core)
                    def _():
                        for half in range(2):
                            sib_copy(step, slot, half).wait_recv()
                        multiply_part(step, slot, 0)

                sib_left(step, 1).wait_recv()
                for slot in (0, 1, 7):
                    @pl.when(user(z, slot) == core)
                    def _():
                        multiply_part(step, slot, 1)
            else:
                for slot in (stage, 8 - stage):
                    @pl.when(user(z, slot) == core)
                    def _():
                        for half in range(2):
                            if last(slot, half):
                                for lane in range(2):
                                    ring_arrival(step, lane, slot, half).wait_recv()
                            else:
                                sib_copy(step, slot, half).wait_recv()
                        multiply(step, slot)

        @pl.when(user(z, 4) == core)
        def _():
            for lane in range(2):
                for half in range(2):
                    ring_arrival(step, lane, 4, half).wait_recv()
            multiply(step, 4)

        @pl.when(jnp.logical_and(step == 0, yh != yl))
        def _():
            swap.wait_recv()

        mine = lax.rem(x - z + 8, 4)
        for half in range(2):
            total = outgoing[step, mine, 0, rows(half)].astype(jnp.float32)
            for slot in range(1, 8):
                here = incoming.at[step, slot, rows(half)]
                remote(
                    here, here, sum_send.at[step, 0, 0, half], sum_recv.at[step, slot, half], sibling
                ).wait_recv()
                total += incoming[step, slot, rows(half)].astype(jnp.float32)
            square = select_block(square_ref[row_, block_], total)

            @pl.when(step == 0)
            def _():
                following = 2.0 * swapped[rows(half)].astype(jnp.float32) - square
                left[1, 0, rows(half)] = following.astype(jnp.bfloat16)
                for slot in (1, 7):
                    ring_copy(1, slot, half).start()

            @pl.when(step != 0)
            def _():
                out_block[rows(half)] = square.astype(jnp.bfloat16)
                out_copy(half).start()

    @pl.loop(0, STEPS)
    def _(step):
        for slot in range(1, 8):
            for half in range(2):
                ring_copy(step, slot, half).wait_send()
                if not last(slot, half):
                    @pl.when(user(z, slot) != core)
                    def _():
                        sib_copy(step, slot, half).wait_send()
        far_copy(step).wait_send()
        for part in range(2):
            sib_left(step, part).wait_send()
        for pair in range(4):
            for half in range(2):
                sum_copy(step, pair, 1, half).wait_send()

                @pl.when(elsewhere(pair))
                def _():
                    sum_copy(step, pair, 0, half).wait_send()

    @pl.when(yh != yl)
    def _():
        swap.wait_send()

    for half in range(2):
        out_copy(half).wait()


def local(density, pattern_start, pattern_square):
    block = (BLOCK, BLOCK)
    kind = jnp.bfloat16
    dma = pltpu.SemaphoreType.DMA
    return pl.pallas_call(
        kernel,
        name="purify",
        out_shape=jax.ShapeDtypeStruct(block, kind),
        in_specs=[pl.BlockSpec(memory_space=pl.ANY)] * 3,
        out_specs=pl.BlockSpec(memory_space=pl.ANY),
        scratch_shapes=[
            pltpu.VMEM(block, kind),
            pltpu.SMEM(pattern_start.shape, jnp.int32),
            pltpu.SMEM(pattern_square.shape, jnp.int32),
            dma((3,)),
            pltpu.VMEM((STEPS, 2, 2 * BLOCK, BLOCK), kind),
            pltpu.VMEM((STEPS, 2, 8) + block, kind),
            pltpu.VMEM((STEPS, 4, 2) + block, kind),
            pltpu.VMEM((STEPS, 8) + block, kind),
            pltpu.VMEM(block, kind),
            dma((STEPS, 8, 2)), dma((STEPS, 2, 8, 2)),
            dma((STEPS, 8, 2)), dma((STEPS, 8, 2)),
            dma((STEPS,)), dma((STEPS,)),
            dma((STEPS, 4, 2, 2)), dma((STEPS, 8, 2)),
            dma(()), dma(()),
            pltpu.SemaphoreType.REGULAR, dma((2,)), pltpu.VMEM(block, kind),
        ],
        compiler_params=pltpu.CompilerParams(
            collective_id=0, has_side_effects=True, vmem_limit_bytes=62 * 2**20
        ),
    )(pattern_start, pattern_square, density)


def solution(mesh):
    return jax.shard_map(
        local,
        mesh=mesh,
        in_specs=(P("row", ("col", "ka")), P(), P()),
        out_specs=P("row", ("col", "ka")),
        check_vma=False,
    )
```
